32 devices in a mesh: grp: 4 (over x, core), dom: 8 (over z, y).
Axes of the slice: x: 2, y: 2, z: 4, core: 2. Of those that a mesh axis runs over, the one named last changes fastest.
Arguments:
- emb: bfloat16 [8, 4096, 256], P('dom', 'grp'), may hold values from -4.5 to 4.5
- rel: float32 [256], replicated, may hold values from 0.5 to 2
- round_key: int32 [1], replicated, may hold values from 1 to 7
- edge_src: int32 [4, 8, 16, 128], P('grp', 'dom'), may hold values from 0 to 4095
- edge_dst: int32 [4, 8, 16, 128], P('grp', 'dom'), may hold values from 0 to 4095
- neg_idx: int32 [4, 8, 16, 128], P('grp', 'dom'), may hold values from 0 to 4095
- block_count: int32 [4, 8, 2], P('grp', 'dom'), may hold values from 1 to 8
Outputs:
- emb_grad: float32 [8, 4096, 256], P('dom', 'grp')
The draws below stay inside these ranges and needn't reach their ends.
Inputs may be any that keep to these rules, and one draw needn't show every extreme that they name: Partition p is matched with partition p XOR round_key[0]; round_key is the same on every device. `edge_src`: row numbers within a partition. `edge_dst`: row numbers within a partition. `neg_idx`: row numbers within a partition.
All inputs are finite; a program needn't handle non-finite values.
Results may differ from the reference program's by a relative error of at most 0.009.
Values may be sent and summed in bfloat16 or wider, within the bound.
A program may use at most 64 MiB of HBM per device.

```python
import math
import jax
import jax.numpy as jnp
from jax import lax

D = 256
NB = 8
EB = 128
PROWS = 4096
N_GRP = 4
N_DOM = 8


def draw_emb(key, part):
    first = jax.random.fold_in(key, 0)
    shape = (N_DOM, PROWS, D)
    values = jnp.clip(jax.random.normal(first, shape, jnp.float32), -4.0, 4.0)
    return jnp.clip(values, -4.5, 4.5).astype(jnp.bfloat16)


def place_ends(array, rng, low, largest):
    place = [jax.random.randint(jax.random.fold_in(rng, axis), (), 0, length) for axis, length in enumerate(array.shape)]
    longest = array.shape.index(max(array.shape))
    next_to = place[:longest] + [(place[longest] + 1) % array.shape[longest]] + place[longest + 1:]
    return array.at[tuple(place)].set(low).at[tuple(next_to)].set(largest)


def setup_inputs(seed: int = 0) -> dict:
    keys = jax.random.split(jax.random.key(seed), 8)
    return {
        "emb": draw_emb(jax.random.fold_in(keys[7], 71), 0),
        "rel": jnp.clip(jnp.exp(jax.random.uniform(keys[1], (D,), jnp.float32, math.log(0.5), math.log(2.0))), 0.5, 2.0),
        "round_key": jax.random.randint(keys[2], (1,), 1, N_DOM).astype(jnp.int32),
        "edge_src": place_ends(jax.random.randint(keys[3], (N_GRP, N_DOM, 2 * NB, EB), 0, PROWS), jax.random.fold_in(keys[3], 1), 0, PROWS - 1).astype(jnp.int32),
        "edge_dst": place_ends(jax.random.randint(keys[4], (N_GRP, N_DOM, 2 * NB, EB), 0, PROWS), jax.random.fold_in(keys[4], 1), 0, PROWS - 1).astype(jnp.int32),
        "neg_idx": place_ends(jax.random.randint(keys[5], (N_GRP, N_DOM, 2 * NB, EB), 0, PROWS), jax.random.fold_in(keys[5], 1), 0, PROWS - 1).astype(jnp.int32),
        "block_count": place_ends(jax.random.randint(keys[6], (N_GRP, N_DOM, 2), 1, NB + 1), jax.random.fold_in(keys[6], 1), 1, NB).astype(jnp.int32),
    }


def bucket_terms(src_table, dst_table, rel, src_idx, dst_idx, neg_idx, count):
    scale = D ** -0.5
    src_rows = src_table[src_idx]
    dst_rows = dst_table[dst_idx]
    neg_rows = dst_table[neg_idx]
    query = lax.optimization_barrier((src_rows * rel * scale).astype(jnp.bfloat16)).astype(jnp.float32)
    cand = jnp.concatenate([dst_rows, neg_rows], axis=1)
    logits = jnp.einsum('bed,bcd->bec', query, cand)
    probs = jax.nn.softmax(logits, axis=-1)
    live = (jnp.arange(NB, dtype=jnp.int32) < count).astype(jnp.float32)
    target = jnp.eye(EB, 2 * EB, dtype=jnp.float32)
    weights = ((probs - target) * live[:, None, None]).astype(jnp.bfloat16).astype(jnp.float32)
    grad_query = jnp.einsum('bec,bcd->bed', weights, cand)
    src_grad = (grad_query * rel * scale).astype(jnp.bfloat16).astype(jnp.float32)
    cand_grad = jnp.einsum('bec,bed->bcd', weights, query).astype(jnp.bfloat16).astype(jnp.float32)
    own = jnp.zeros((PROWS, D), jnp.float32).at[src_idx.reshape(-1)].add(src_grad.reshape(-1, D))
    far = jnp.zeros((PROWS, D), jnp.float32).at[dst_idx.reshape(-1)].add(cand_grad[:, :EB].reshape(-1, D))
    far = far.at[neg_idx.reshape(-1)].add(cand_grad[:, EB:].reshape(-1, D))
    return own, far


def reference(emb, rel, round_key, edge_src, edge_dst, neg_idx, block_count):
    table = emb.astype(jnp.float32)
    parts = jnp.arange(N_DOM, dtype=jnp.int32)
    partner = jnp.bitwise_xor(parts, round_key[0].astype(jnp.int32))

    def per_part(index):
        own_tab = table[index]
        mate_tab = table[partner[index]]

        def per_group(sources, targets, negatives, counts):
            own_a, far_a = bucket_terms(own_tab, own_tab, rel, sources[:NB], targets[:NB], negatives[:NB], counts[0])
            own_b, far_b = bucket_terms(own_tab, mate_tab, rel, sources[NB:], targets[NB:], negatives[NB:], counts[1])
            return own_a + own_b + far_a, far_b

        own_g, mate_g = jax.vmap(per_group)(edge_src[:, index], edge_dst[:, index], neg_idx[:, index], block_count[:, index])
        return jnp.sum(own_g, axis=0), jnp.sum(mate_g, axis=0)

    own_all, mate_all = lax.map(per_part, parts)
    return own_all + mate_all[partner]
```

```python
import jax
import jax.numpy as jnp
from jax import lax
from jax.sharding import PartitionSpec as P


def swap_with_mate(arrays, key):
    count = lax.axis_size("dom")

    def branch(k):
        route = [(p, p ^ k) for p in range(count)]
        return lambda xs: tuple(lax.ppermute(x, "dom", route) for x in xs)

    return lax.switch(key - 1, [branch(k) for k in range(1, count)], arrays)


def onehot_rows(idx, rows):
    flat = idx.reshape(-1)
    return (flat[:, None] == jnp.arange(rows, dtype=jnp.int32)[None, :]).astype(jnp.bfloat16)


def pick(idx, table):
    return jnp.dot(
        onehot_rows(idx, table.shape[0]), table, preferred_element_type=jnp.float32
    ).astype(jnp.bfloat16)


def make_query(idx, table, rel):
    rows = pick(idx, table)
    scale = table.shape[1] ** (-0.5)
    return (rows.astype(jnp.float32) * rel * scale).astype(jnp.bfloat16)


def score(query, table, rel, dst, neg, count):
    blocks, width = dst.shape
    depth = table.shape[1]
    scale = depth ** (-0.5)
    query = query.reshape(blocks, width, depth)
    cand = jnp.concatenate(
        [pick(dst, table).reshape(blocks, width, depth), pick(neg, table).reshape(blocks, width, depth)],
        axis=1,
    )
    logits = jnp.einsum("bed,bcd->bec", query, cand, preferred_element_type=jnp.float32)
    probs = jax.nn.softmax(logits, axis=-1)
    live = (jnp.arange(blocks, dtype=jnp.int32) < count).astype(jnp.float32)
    target = jnp.eye(width, 2 * width, dtype=jnp.float32)
    weights = ((probs - target) * live[:, None, None]).astype(jnp.bfloat16)
    grad_query = jnp.einsum("bec,bcd->bed", weights, cand, preferred_element_type=jnp.float32)
    src_grad = (grad_query * rel * scale).astype(jnp.bfloat16).reshape(-1, depth)
    cand_grad = jnp.einsum(
        "bec,bed->bcd", weights, query, preferred_element_type=jnp.float32
    ).astype(jnp.bfloat16)
    return src_grad, cand_grad[:, :width].reshape(-1, depth), cand_grad[:, width:].reshape(-1, depth)


def spread(idx, grads, rows):
    return jnp.einsum(
        "rp,rd->pd", onehot_rows(idx, rows), grads, preferred_element_type=jnp.float32
    )


def on_device(emb, rel, round_key, edge_src, edge_dst, neg_idx, block_count):
    key = round_key[0]
    table = lax.all_gather(emb[0], "grp", axis=0, tiled=True)
    rows = table.shape[0]
    src, dst, neg, counts = edge_src[0, 0], edge_dst[0, 0], neg_idx[0, 0], block_count[0, 0]
    blocks = src.shape[0] // 2
    query_b = make_query(src[blocks:], table, rel)
    query_in, dst_in, neg_in, count_in = swap_with_mate(
        (query_b, dst[blocks:], neg[blocks:], counts[1:]), key
    )
    query_a = make_query(src[:blocks], table, rel)
    sgrad_a, dgrad_a, ngrad_a = score(query_a, table, rel, dst[:blocks], neg[:blocks], counts[0])
    sgrad_in, dgrad_in, ngrad_in = score(query_in, table, rel, dst_in, neg_in, count_in[0])
    (sgrad_b,) = swap_with_mate((sgrad_in,), key)
    total = spread(src[:blocks], sgrad_a, rows) + spread(dst[:blocks], dgrad_a, rows)
    total += spread(neg[:blocks], ngrad_a, rows) + spread(dst_in, dgrad_in, rows)
    total += spread(neg_in, ngrad_in, rows) + spread(src[blocks:], sgrad_b, rows)
    return lax.psum_scatter(total[None], "grp", scatter_dimension=1, tiled=True)


def solution(mesh):
    return jax.shard_map(
        on_device,
        mesh=mesh,
        in_specs=(
            P("dom", "grp", None),
            P(),
            P(),
            P("grp", "dom", None, None),
            P("grp", "dom", None, None),
            P("grp", "dom", None, None),
            P("grp", "dom", None),
        ),
        out_specs=P("dom", "grp", None),
        check_vma=False,
    )
```

```python
import jax
import jax.numpy as jnp
from jax import lax
from jax.experimental import pallas as pl
from jax.experimental.pallas import tpu as pltpu
from jax.sharding import PartitionSpec as P

MESH = pl.DeviceIdType.MESH
F32 = jnp.float32
BF16 = jnp.bfloat16
STEP = 1024
GROUP = 4
PIECES = 4
VMEM = pl.BlockSpec(memory_space=pltpu.VMEM)
SMEM = pl.BlockSpec(memory_space=pltpu.SMEM)
LIMIT = 48 * 1024 * 1024


def grp_peers():
    g = lax.axis_index("grp")
    sib = g + 1 - 2 * lax.rem(g, 2)
    far = lax.rem(g + 2, 4)
    both = lax.rem(sib + 2, 4)
    return g, sib, far, both


def meet(peers):
    barrier = pltpu.get_barrier_semaphore()
    for peer in peers:
        pl.semaphore_signal(barrier, inc=1, device_id={"grp": peer}, device_id_type=MESH)
    pl.semaphore_wait(barrier, len(peers))


def columns(idx_t, first, blocks):
    lane = lax.broadcasted_iota(jnp.int32, idx_t.shape, 1)
    cols = [
        jnp.sum(jnp.where(lane == first + j, idx_t, 0.0), axis=1, keepdims=True)
        for j in range(blocks)
    ]
    return jnp.concatenate(cols, axis=0).astype(jnp.int32)


def pick_step(col, base, rows_ref):
    depth = rows_ref.shape[0]
    lane = lax.broadcasted_iota(jnp.int32, (col.shape[0], depth), 1)
    hot = jnp.where(lane == col - base, 1.0, 0.0).astype(BF16)
    return jnp.dot(hot, rows_ref[...], preferred_element_type=F32)


def spread_step(idx_rows, base, tile, grads):
    line = jnp.concatenate([idx_rows[j : j + 1, :] for j in range(idx_rows.shape[0])], axis=1)
    sub = lax.broadcasted_iota(jnp.int32, (tile, line.shape[1]), 0)
    hot = jnp.where(sub == line - base, 1.0, 0.0).astype(BF16)
    return jnp.dot(hot, grads, preferred_element_type=F32)


def score_block(query, cand, rel, live):
    width, depth = query.shape
    logits = lax.dot_general(query, cand, (((1,), (1,)), ((), ())), preferred_element_type=F32)
    top = jnp.max(logits, axis=1, keepdims=True)
    expd = jnp.exp(logits - top)
    probs = expd / jnp.sum(expd, axis=1, keepdims=True)
    row = lax.broadcasted_iota(jnp.int32, logits.shape, 0)
    col = lax.broadcasted_iota(jnp.int32, logits.shape, 1)
    weights = (probs - jnp.where(row == col, 1.0, 0.0)) * live
    weights_t = jnp.transpose(weights).astype(BF16)
    weights = weights.astype(BF16)
    grad_query = jnp.dot(weights, cand, preferred_element_type=F32)
    src_grad = (grad_query * rel * depth ** (-0.5)).astype(BF16)
    cand_grad = jnp.dot(weights_t, query, preferred_element_type=F32).astype(BF16)
    return src_grad, cand_grad


def gather_kernel(emb_ref, src_ref, rel_ref, table_ref, query_ref, acc_ref,
                  own_send, own_recv, far_send, far_recv, fwd_send, fwd_recv, keep_sem):
    g, sib, far, both = grp_peers()
    shard, depth = emb_ref.shape
    piece = shard // PIECES
    meet([sib, far])
    far_copies = []
    for c in range(PIECES):
        part = pl.ds(c * piece, piece)
        copy = pltpu.make_async_remote_copy(
            src_ref=emb_ref.at[part], dst_ref=table_ref.at[g, part],
            send_sem=far_send.at[c], recv_sem=far_recv.at[c],
            device_id={"grp": far}, device_id_type=MESH)
        copy.start()
        far_copies.append(copy)
    own = pltpu.make_async_remote_copy(
        src_ref=emb_ref, dst_ref=table_ref.at[g], send_sem=own_send, recv_sem=own_recv,
        device_id={"grp": sib}, device_id_type=MESH)
    own.start()
    keep = pltpu.make_async_copy(emb_ref, table_ref.at[g], keep_sem)
    keep.start()
    idx_t = jnp.transpose(src_ref[...].astype(F32))
    blocks = src_ref.shape[0]
    rows = GROUP * src_ref.shape[1]

    def take(s, rows_ref, first):
        for i in range(blocks // GROUP):
            part = pl.ds(i * rows, rows)
            got = pick_step(columns(idx_t, i * GROUP, GROUP), s * shard, rows_ref)
            acc_ref[part] = got if first else acc_ref[part] + got

    take(g, emb_ref, True)
    own.wait()
    take(sib, table_ref.at[sib], False)
    fwd_copies = []
    for c in range(PIECES):
        part = pl.ds(c * piece, piece)
        far_copies[c].wait()
        copy = pltpu.make_async_remote_copy(
            src_ref=table_ref.at[far, part], dst_ref=table_ref.at[far, part],
            send_sem=fwd_send.at[c], recv_sem=fwd_recv.at[c],
            device_id={"grp": sib}, device_id_type=MESH)
        copy.start()
        fwd_copies.append(copy)
    take(far, table_ref.at[far], False)
    for copy in fwd_copies:
        copy.wait()
    take(both, table_ref.at[both], False)
    query_ref[...] = (acc_ref[...] * rel_ref[...] * depth ** (-0.5)).astype(BF16)
    keep.wait()


def gather_and_query(emb, src, rel):
    shard, depth = emb.shape
    dma = pltpu.SemaphoreType.DMA
    entries = src.size
    return pl.pallas_call(
        gather_kernel,
        out_shape=(
            jax.ShapeDtypeStruct((4, shard, depth), BF16),
            jax.ShapeDtypeStruct((entries, depth), BF16),
        ),
        in_specs=[VMEM] * 3,
        out_specs=(VMEM, VMEM),
        scratch_shapes=[
            pltpu.VMEM((entries, depth), F32),
            dma, dma, dma((PIECES,)), dma((PIECES,)), dma((PIECES,)), dma((PIECES,)), dma,
        ],
        compiler_params=pltpu.CompilerParams(
            collective_id=0, has_side_effects=True, vmem_limit_bytes=LIMIT
        ),
        cost_estimate=pl.CostEstimate(
            flops=2 * entries * 4 * shard * depth, bytes_accessed=8 * shard * depth, transcendentals=0
        ),
    )(emb, src, rel)


def pick_kernel(count_ref, idx_ref, table_ref, rel_ref, grads_ref, cand_ref, idx_t_ref, rows_ref):
    idx_t_ref[...] = jnp.transpose(idx_ref[...].astype(F32))
    width = idx_ref.shape[1]
    shards, shard, depth = table_ref.shape
    blocks = grads_ref.shape[0] // (3 * width)
    entries = blocks * width
    tile = GROUP * width

    @pl.loop(0, idx_ref.shape[0] // GROUP)
    def _(i):
        col = columns(idx_t_ref[...], i * GROUP, GROUP)

        def body(s, acc):
            return acc + pick_step(col, s * shard, table_ref.at[s])

        acc = lax.fori_loop(0, shards, body, jnp.zeros((tile, depth), F32))
        rows_ref[pl.ds(pl.multiple_of(i * tile, tile), tile)] = acc.astype(BF16)

    cand_ref[...] = rows_ref[3 * entries :, :]
    rel = rel_ref[...]

    @pl.loop(0, blocks // 2)
    def _(pair):
        for b in (2 * pair, 2 * pair + 1):
            at = pl.multiple_of(b * width, width)
            src_at = pl.ds(at, width)
            dst_at = pl.ds(at + entries, width)
            neg_at = pl.ds(at + 2 * entries, width)
            query = (rows_ref[src_at].astype(F32) * rel * depth ** (-0.5)).astype(BF16)
            cand = jnp.concatenate([rows_ref[dst_at], rows_ref[neg_at]], axis=0)
            live = jnp.where(b < count_ref[0], 1.0, 0.0)
            src_grad, cand_grad = score_block(query, cand, rel, live)
            grads_ref[src_at] = src_grad
            grads_ref[dst_at] = cand_grad[:width]
            grads_ref[neg_at] = cand_grad[width:]


def pick_and_score(count, idx, table, rel):
    width = idx.shape[1]
    shards, shard, depth = table.shape
    total = idx.size
    entries = total // 5
    return pl.pallas_call(
        pick_kernel,
        out_shape=(
            jax.ShapeDtypeStruct((3 * entries, depth), BF16),
            jax.ShapeDtypeStruct((2 * entries, depth), BF16),
        ),
        in_specs=[SMEM, VMEM, VMEM, VMEM],
        out_specs=(VMEM, VMEM),
        scratch_shapes=[pltpu.VMEM((width, idx.shape[0]), F32), pltpu.VMEM((total, depth), BF16)],
        compiler_params=pltpu.CompilerParams(vmem_limit_bytes=LIMIT),
        cost_estimate=pl.CostEstimate(
            flops=2 * total * shards * shard * depth, bytes_accessed=6 * total * depth, transcendentals=0
        ),
    )(count, idx, table, rel)


def score_kernel(count_ref, query_ref, cand_ref, rel_ref, src_out, cand_out):
    rel = rel_ref[...]
    entries = query_ref.shape[0]
    width = 128
    blocks = entries // width

    @pl.loop(0, blocks // 2)
    def _(pair):
        for b in (2 * pair, 2 * pair + 1):
            at = pl.multiple_of(b * width, width)
            dst_at = pl.ds(at, width)
            neg_at = pl.ds(at + entries, width)
            cand = jnp.concatenate([cand_ref[dst_at], cand_ref[neg_at]], axis=0)
            live = jnp.where(b < count_ref[0], 1.0, 0.0)
            src_grad, cand_grad = score_block(query_ref[dst_at], cand, rel, live)
            src_out[dst_at] = src_grad
            cand_out[dst_at] = cand_grad[:width]
            cand_out[neg_at] = cand_grad[width:]


def score_in(count, query, cand, rel):
    return pl.pallas_call(
        score_kernel,
        out_shape=(
            jax.ShapeDtypeStruct(query.shape, BF16),
            jax.ShapeDtypeStruct(cand.shape, BF16),
        ),
        in_specs=[SMEM, VMEM, VMEM, VMEM],
        out_specs=(VMEM, VMEM),
        compiler_params=pltpu.CompilerParams(vmem_limit_bytes=LIMIT),
    )(count, query, cand, rel)


def spread_kernel(idx_ref, near_ref, cand_ref, out_ref):
    shards, shard, depth = out_ref.shape
    width = idx_ref.shape[1]
    blocks = STEP // width
    tile = 512
    tiles = shard // tile

    @pl.loop(0, shards * tiles)
    def _(t):
        def add(ref, skip):
            def body(k, acc):
                at = pl.ds(pl.multiple_of(k * STEP, STEP), STEP)
                idx = idx_ref[pl.ds(pl.multiple_of(k * blocks, blocks) + skip, blocks)]
                return acc + spread_step(idx, t * tile, tile, ref[at])

            return body

        near_steps = near_ref.shape[0] // STEP
        acc = jnp.zeros((tile, depth), F32)
        acc = lax.fori_loop(0, near_steps, add(near_ref, 0), acc)
        acc = lax.fori_loop(0, cand_ref.shape[0] // STEP, add(cand_ref, near_steps * blocks), acc)
        at = pl.ds(pl.multiple_of(lax.rem(t, tiles) * tile, tile), tile)
        out_ref[lax.div(t, tiles), at] = acc


def spread_most(idx, near, cand, shards, shard):
    depth = near.shape[1]
    total = idx.size
    return pl.pallas_call(
        spread_kernel,
        out_shape=jax.ShapeDtypeStruct((shards, shard, depth), F32),
        in_specs=[VMEM] * 3,
        out_specs=VMEM,
        compiler_params=pltpu.CompilerParams(vmem_limit_bytes=LIMIT),
        cost_estimate=pl.CostEstimate(
            flops=2 * total * shards * shard * depth, bytes_accessed=8 * total * depth, transcendentals=0
        ),
    )(idx, near, cand)


def reduce_kernel(most_ref, src_ref, grad_ref, out_ref, to_sib, from_sib, to_far, from_far,
                  sib_send, sib_recv, far_send, far_recv):
    g, sib, far, both = grp_peers()
    shards, shard, depth = most_ref.shape
    piece = shard // PIECES
    meet([sib, far])
    idx = src_ref[...]

    def part_sum(s, c):
        near = spread_step(idx, s * shard + c * piece, piece, grad_ref[...])
        return most_ref[s, pl.ds(c * piece, piece)] + near

    sib_copies = []
    for slot, s in ((0, both), (1, sib)):
        for c in range(PIECES):
            part = pl.ds(c * piece, piece)
            to_sib[slot, part] = part_sum(s, c).astype(BF16)
            copy = pltpu.make_async_remote_copy(
                src_ref=to_sib.at[slot, part], dst_ref=from_sib.at[slot, part],
                send_sem=sib_send.at[slot, c], recv_sem=sib_recv.at[slot, c],
                device_id={"grp": sib}, device_id_type=MESH)
            copy.start()
            sib_copies.append(copy)
        if slot == 0:
            far_copies = []
            for c in range(PIECES):
                part = pl.ds(c * piece, piece)
                mine = part_sum(far, c)
                sib_copies[c].wait()
                to_far[part] = (mine + from_sib[0, part].astype(F32)).astype(BF16)
                copy = pltpu.make_async_remote_copy(
                    src_ref=to_far.at[part], dst_ref=from_far.at[part],
                    send_sem=far_send.at[c], recv_sem=far_recv.at[c],
                    device_id={"grp": far}, device_id_type=MESH)
                copy.start()
                far_copies.append(copy)
    for c in range(PIECES):
        part = pl.ds(c * piece, piece)
        mine = part_sum(g, c)
        sib_copies[PIECES + c].wait()
        out_ref[part] = mine + from_sib[1, part].astype(F32)
    for c in range(PIECES):
        part = pl.ds(c * piece, piece)
        far_copies[c].wait()
        out_ref[part] = out_ref[part] + from_far[part].astype(F32)


def spread_and_reduce(most, src, grad):
    shards, shard, depth = most.shape
    dma = pltpu.SemaphoreType.DMA
    return pl.pallas_call(
        reduce_kernel,
        out_shape=jax.ShapeDtypeStruct((shard, depth), F32),
        in_specs=[VMEM] * 3,
        out_specs=VMEM,
        scratch_shapes=[
            pltpu.VMEM((2, shard, depth), BF16), pltpu.VMEM((2, shard, depth), BF16),
            pltpu.VMEM((shard, depth), BF16), pltpu.VMEM((shard, depth), BF16),
            dma((2, PIECES)), dma((2, PIECES)), dma((PIECES,)), dma((PIECES,)),
        ],
        compiler_params=pltpu.CompilerParams(
            collective_id=1, has_side_effects=True, vmem_limit_bytes=LIMIT
        ),
    )(most, src, grad)


def on_device(emb, rel, round_key, edge_src, edge_dst, neg_idx, block_count):
    key = round_key[0]
    count_dom = lax.axis_size("dom")
    routes = [[(p, p ^ k) for p in range(count_dom)] for k in range(1, count_dom)]
    rel = rel[None]
    src, dst, neg, counts = edge_src[0, 0], edge_dst[0, 0], neg_idx[0, 0], block_count[0, 0]
    blocks, width = src.shape[0] // 2, src.shape[1]
    mail = jnp.concatenate(
        [dst[blocks:], neg[blocks:], jnp.broadcast_to(counts[1], (blocks, width))], axis=0
    )
    mails = lax.all_gather(mail, "dom", axis=0)
    table, query_b = gather_and_query(emb[0], src[blocks:], rel)
    mate = jnp.bitwise_xor(lax.axis_index("dom"), key)
    mail_in = lax.dynamic_index_in_dim(mails, mate, axis=0, keepdims=False)
    idx_most = jnp.concatenate(
        [src[:blocks], dst[:blocks], neg[:blocks], mail_in[: 2 * blocks]], axis=0
    )

    def out_way(route):
        def run(query, count, idx, table, rel):
            moved = lax.ppermute(query, "dom", route)
            return (moved,) + tuple(pick_and_score(count, idx, table, rel))

        return run

    query_in, near_grads, cand_in = lax.switch(
        key - 1, [out_way(r) for r in routes], query_b, counts[:1], idx_most, table, rel
    )
    sgrad_in, cgrad_in = score_in(mail_in[2 * blocks, :1], query_in, cand_in, rel)

    def back_way(route):
        def run(sgrad, idx, near, cand):
            moved = lax.ppermute(sgrad, "dom", route)
            return moved, spread_most(idx, near, cand, table.shape[0], table.shape[1])

        return run

    sgrad_b, most = lax.switch(
        key - 1, [back_way(r) for r in routes], sgrad_in, idx_most, near_grads, cgrad_in
    )
    return spread_and_reduce(most, src[blocks:], sgrad_b)[None]


def solution(mesh):
    return jax.shard_map(
        on_device,
        mesh=mesh,
        in_specs=(
            P("dom", "grp", None),
            P(),
            P(),
            P("grp", "dom", None, None),
            P("grp", "dom", None, None),
            P("grp", "dom", None, None),
            P("grp", "dom", None),
        ),
        out_specs=P("dom", "grp", None),
        check_vma=False,
    )
```

```python
import jax
import jax.numpy as jnp
from jax import lax
from jax.experimental import pallas as pl
from jax.experimental.pallas import tpu as pltpu
from jax.sharding import PartitionSpec as P

MESH = pl.DeviceIdType.MESH
F32 = jnp.float32
BF16 = jnp.bfloat16
STEP = 1024
EXACT = 256
PIECES = 4
VMEM = pl.BlockSpec(memory_space=pltpu.VMEM)
SMEM = pl.BlockSpec(memory_space=pltpu.SMEM)
LIMIT = 48 * 1024 * 1024


def grp_peers():
    g = lax.axis_index("grp")
    sib = g + 1 - 2 * lax.rem(g, 2)
    far = lax.rem(g + 2, 4)
    both = lax.rem(sib + 2, 4)
    return g, sib, far, both


def meet(peers):
    barrier = pltpu.get_barrier_semaphore()
    for peer in peers:
        pl.semaphore_signal(barrier, inc=1, device_id={"grp": peer}, device_id_type=MESH)
    pl.semaphore_wait(barrier, len(peers))


def spread_step(idx_rows, base, tile, grads):
    line = jnp.concatenate([idx_rows[j : j + 1, :] for j in range(idx_rows.shape[0])], axis=1)
    parts = []
    for first in range(0, tile, EXACT):
        near = (line - (base + first)).astype(F32).astype(BF16)
        sub = lax.broadcasted_iota(jnp.int32, (EXACT, line.shape[1]), 0).astype(F32).astype(BF16)
        one = jnp.ones(sub.shape, BF16)
        parts.append(jnp.where(sub == near, one, jnp.zeros_like(one)))
    hot = jnp.concatenate(parts, axis=0) if len(parts) > 1 else parts[0]
    return jnp.dot(hot, grads, preferred_element_type=F32)


def load_wide(ref, at):
    return jnp.concatenate([ref[at, 0, :], ref[at, 1, :]], axis=1)


def pick_rows(idx_ref, first, blocks, table_ref, rows_ref, to):
    width = idx_ref.shape[1]
    unroll = 16

    @pl.loop(0, blocks * width // unroll)
    def _(i):
        b = lax.div(i, width // unroll)
        lane = lax.rem(i, width // unroll) * unroll
        for j in range(unroll):
            rows_ref[to + i * unroll + j] = table_ref[idx_ref[first + b, lane + j]]


def score_block(query, cand, rel, live):
    width, depth = query.shape
    logits = lax.dot_general(query, cand, (((1,), (1,)), ((), ())), preferred_element_type=F32)
    top = jnp.max(logits, axis=1, keepdims=True)
    expd = jnp.exp(logits - top)
    probs = expd / jnp.sum(expd, axis=1, keepdims=True)
    row = lax.broadcasted_iota(jnp.int32, logits.shape, 0)
    col = lax.broadcasted_iota(jnp.int32, logits.shape, 1)
    weights = (probs - jnp.where(row == col, 1.0, 0.0)) * live
    weights_t = jnp.transpose(weights).astype(BF16)
    weights = weights.astype(BF16)
    grad_query = jnp.dot(weights, cand, preferred_element_type=F32)
    src_grad = (grad_query * rel * depth ** (-0.5)).astype(BF16)
    cand_grad = jnp.dot(weights_t, query, preferred_element_type=F32).astype(BF16)
    return src_grad, cand_grad


def gather_kernel(emb_ref, dst_ref, neg_ref, count_ref, wide_ref, mails_ref, table_ref, mail_ref,
                  own_send, own_recv, far_send, far_recv, fwd_send, fwd_recv, keep_sem,
                  mail_send, mail_recv):
    g, sib, far, both = grp_peers()
    d = lax.axis_index("dom")
    count_dom = mails_ref.shape[0]
    shard, depth = emb_ref.shape
    half = depth // 2
    piece = shard // PIECES
    blocks = dst_ref.shape[0] // 2
    barrier = pltpu.get_barrier_semaphore()
    for peer in (sib, far):
        pl.semaphore_signal(barrier, inc=1, device_id={"grp": peer}, device_id_type=MESH)
    for j in range(1, count_dom):
        pl.semaphore_signal(
            barrier, inc=1, device_id={"dom": lax.rem(d + j, count_dom)}, device_id_type=MESH
        )
    mail_ref[:blocks] = dst_ref[blocks:]
    mail_ref[blocks : 2 * blocks] = neg_ref[blocks:]
    mail_ref[2 * blocks :] = jnp.broadcast_to(count_ref[:, 1:2], (blocks, dst_ref.shape[1]))
    mails_ref[d] = mail_ref[...]
    keep = pltpu.make_async_copy(emb_ref, table_ref.at[g], keep_sem)
    keep.start()
    pl.semaphore_wait(barrier, 1 + count_dom)
    far_copies = []
    for c in range(PIECES):
        part = pl.ds(c * piece, piece)
        copy = pltpu.make_async_remote_copy(
            src_ref=emb_ref.at[part], dst_ref=table_ref.at[g, part],
            send_sem=far_send.at[c], recv_sem=far_recv.at[c],
            device_id={"grp": far}, device_id_type=MESH)
        copy.start()
        far_copies.append(copy)
    own = pltpu.make_async_remote_copy(
        src_ref=emb_ref, dst_ref=table_ref.at[g], send_sem=own_send, recv_sem=own_recv,
        device_id={"grp": sib}, device_id_type=MESH)
    own.start()
    mail_copies = []
    for j in range(1, count_dom):
        copy = pltpu.make_async_remote_copy(
            src_ref=mail_ref, dst_ref=mails_ref.at[d],
            send_sem=mail_send.at[j], recv_sem=mail_recv.at[j],
            device_id={"dom": lax.rem(d + j, count_dom)}, device_id_type=MESH)
        copy.start()
        mail_copies.append(copy)

    def widen(s, c):
        rows = table_ref[s, pl.ds(c * piece, piece)].astype(F32)
        at = pl.ds(pl.multiple_of(s * shard + c * piece, piece), piece)
        wide_ref[at, 0, :] = rows[:, :half]
        wide_ref[at, 1, :] = rows[:, half:]

    keep.wait()
    for c in range(PIECES):
        widen(g, c)
    own.wait()
    for c in range(PIECES):
        widen(sib, c)
    fwd_copies = []
    for c in range(PIECES):
        part = pl.ds(c * piece, piece)
        far_copies[c].wait()
        copy = pltpu.make_async_remote_copy(
            src_ref=table_ref.at[far, part], dst_ref=table_ref.at[far, part],
            send_sem=fwd_send.at[c], recv_sem=fwd_recv.at[c],
            device_id={"grp": sib}, device_id_type=MESH)
        copy.start()
        fwd_copies.append(copy)
        widen(far, c)
    for c in range(PIECES):
        fwd_copies[c].wait()
        widen(both, c)
    for copy in mail_copies:
        copy.wait()


def gather_table(emb, dst, neg, counts, count_dom):
    shard, depth = emb.shape
    dma = pltpu.SemaphoreType.DMA
    mail = (dst.shape[0] // 2 * 3, dst.shape[1])
    return pl.pallas_call(
        gather_kernel,
        out_shape=(
            jax.ShapeDtypeStruct((4 * shard, 2, depth // 2), F32),
            jax.ShapeDtypeStruct((count_dom,) + mail, jnp.int32),
        ),
        in_specs=[pl.BlockSpec(memory_space=pl.ANY)] + [VMEM] * 3,
        out_specs=(VMEM, VMEM),
        scratch_shapes=[
            pltpu.VMEM((4, shard, depth), BF16),
            pltpu.VMEM(mail, jnp.int32),
            dma, dma, dma((PIECES,)), dma((PIECES,)), dma((PIECES,)), dma((PIECES,)), dma,
            dma((count_dom,)), dma((count_dom,)),
        ],
        compiler_params=pltpu.CompilerParams(
            collective_id=0, has_side_effects=True, vmem_limit_bytes=LIMIT
        ),
    )(emb, dst, neg, counts)


def query_kernel(idx_ref, table_ref, rel_ref, query_ref, rows_ref):
    blocks = idx_ref.shape[0] // 2
    depth = query_ref.shape[1]
    pick_rows(idx_ref, blocks, blocks, table_ref, rows_ref, 0)
    for first in range(0, query_ref.shape[0], EXACT):
        at = pl.ds(first, EXACT)
        query_ref[at] = (load_wide(rows_ref, at) * rel_ref[...] * depth ** (-0.5)).astype(BF16)


def make_query(src, table, rel):
    entries = src.size // 2
    depth = rel.shape[1]
    return pl.pallas_call(
        query_kernel,
        out_shape=jax.ShapeDtypeStruct((entries, depth), BF16),
        in_specs=[SMEM, VMEM, VMEM],
        out_specs=VMEM,
        scratch_shapes=[pltpu.VMEM((entries, 2, depth // 2), F32)],
        compiler_params=pltpu.CompilerParams(vmem_limit_bytes=LIMIT),
    )(src, table, rel)


def pick_kernel(count_ref, src_ref, dst_ref, neg_ref, mail_ref, table_ref, rel_ref,
                grads_ref, cand_ref, rows_ref):
    width = src_ref.shape[1]
    blocks = src_ref.shape[0] // 2
    depth = cand_ref.shape[1]
    entries = blocks * width
    pick_rows(src_ref, 0, blocks, table_ref, rows_ref, 0)
    pick_rows(dst_ref, 0, blocks, table_ref, rows_ref, entries)
    pick_rows(neg_ref, 0, blocks, table_ref, rows_ref, 2 * entries)
    pick_rows(mail_ref, 0, 2 * blocks, table_ref, rows_ref, 3 * entries)

    @pl.loop(0, 2 * entries // EXACT)
    def _(i):
        at = pl.multiple_of(i * EXACT, EXACT)
        cand_ref[pl.ds(at, EXACT)] = load_wide(rows_ref, pl.ds(at + 3 * entries, EXACT)).astype(BF16)

    rel = rel_ref[...]

    @pl.loop(0, blocks // 2)
    def _(pair):
        for b in (2 * pair, 2 * pair + 1):
            at = pl.multiple_of(b * width, width)
            src_at = pl.ds(at, width)
            dst_at = pl.ds(at + entries, width)
            neg_at = pl.ds(at + 2 * entries, width)
            query = (load_wide(rows_ref, src_at) * rel * depth ** (-0.5)).astype(BF16)
            cand = jnp.concatenate(
                [load_wide(rows_ref, dst_at), load_wide(rows_ref, neg_at)], axis=0
            ).astype(BF16)
            live = jnp.where(b < count_ref[0, 0], 1.0, 0.0)
            src_grad, cand_grad = score_block(query, cand, rel, live)
            grads_ref[src_at] = src_grad
            grads_ref[dst_at] = cand_grad[:width]
            grads_ref[neg_at] = cand_grad[width:]


def pick_and_score(counts, src, dst, neg, mail, table, rel):
    entries = src.size // 2
    depth = rel.shape[1]
    return pl.pallas_call(
        pick_kernel,
        out_shape=(
            jax.ShapeDtypeStruct((3 * entries, depth), BF16),
            jax.ShapeDtypeStruct((2 * entries, depth), BF16),
        ),
        in_specs=[SMEM] * 5 + [VMEM] * 2,
        out_specs=(VMEM, VMEM),
        scratch_shapes=[pltpu.VMEM((5 * entries, 2, depth // 2), F32)],
        compiler_params=pltpu.CompilerParams(vmem_limit_bytes=LIMIT),
        cost_estimate=pl.CostEstimate(
            flops=10 * table.size * entries, bytes_accessed=30 * entries * depth, transcendentals=0
        ),
    )(counts, src, dst, neg, mail, table, rel)


def score_kernel(count_ref, query_ref, cand_ref, rel_ref, src_out, cand_out):
    rel = rel_ref[...]
    entries = query_ref.shape[0]
    width = count_ref.shape[1]
    blocks = entries // width

    @pl.loop(0, blocks // 2)
    def _(pair):
        for b in (2 * pair, 2 * pair + 1):
            at = pl.multiple_of(b * width, width)
            dst_at = pl.ds(at, width)
            neg_at = pl.ds(at + entries, width)
            cand = jnp.concatenate([cand_ref[dst_at], cand_ref[neg_at]], axis=0)
            live = jnp.where(b < count_ref[2 * blocks, 0], 1.0, 0.0)
            src_grad, cand_grad = score_block(query_ref[dst_at], cand, rel, live)
            src_out[dst_at] = src_grad
            cand_out[dst_at] = cand_grad[:width]
            cand_out[neg_at] = cand_grad[width:]


def score_in(count, query, cand, rel):
    return pl.pallas_call(
        score_kernel,
        out_shape=(
            jax.ShapeDtypeStruct(query.shape, BF16),
            jax.ShapeDtypeStruct(cand.shape, BF16),
        ),
        in_specs=[SMEM, VMEM, VMEM, VMEM],
        out_specs=(VMEM, VMEM),
        compiler_params=pltpu.CompilerParams(vmem_limit_bytes=LIMIT),
    )(count, query, cand, rel)


def spread_kernel(src_ref, dst_ref, neg_ref, mail_ref, near_ref, cand_ref, out_ref):
    shards, shard, depth = out_ref.shape
    blocks = src_ref.shape[0] // 2
    entries = blocks * src_ref.shape[1]
    tile = 512
    tiles = shard // tile

    @pl.loop(0, shards * tiles)
    def _(t):
        base = t * tile
        acc = jnp.zeros((tile, depth), F32)
        for i, ref in enumerate((src_ref, dst_ref, neg_ref)):
            grads = near_ref[i * entries : (i + 1) * entries]
            acc += spread_step(ref[:blocks], base, tile, grads)
        for i in range(2):
            grads = cand_ref[i * entries : (i + 1) * entries]
            acc += spread_step(mail_ref[i * blocks : (i + 1) * blocks], base, tile, grads)
        at = pl.ds(pl.multiple_of(lax.rem(t, tiles) * tile, tile), tile)
        out_ref[lax.div(t, tiles), at] = acc


def spread_most(src, dst, neg, mail, near, cand, shards, shard):
    entries, depth = near.shape[0] // 3, near.shape[1]
    return pl.pallas_call(
        spread_kernel,
        out_shape=jax.ShapeDtypeStruct((shards, shard, depth), F32),
        in_specs=[VMEM] * 6,
        out_specs=VMEM,
        compiler_params=pltpu.CompilerParams(vmem_limit_bytes=LIMIT),
        cost_estimate=pl.CostEstimate(
            flops=10 * entries * shards * shard * depth, bytes_accessed=40 * entries * depth,
            transcendentals=0,
        ),
    )(src, dst, neg, mail, near, cand)


def reduce_kernel(total_ref, src_ref, grad_ref, out_ref, most_ref, most_sem, to_sib, from_sib, to_far, from_far,
                  sib_send, sib_recv, far_send, far_recv):
    g, sib, far, both = grp_peers()
    shards, shard, depth = most_ref.shape
    piece = shard // PIECES
    blocks = src_ref.shape[0] // 2
    loads = {}
    for i, s in enumerate((both, far, sib, g)):
        loads[i] = pltpu.make_async_copy(total_ref.at[s], most_ref.at[s], most_sem.at[i])
        loads[i].start()
    meet([sib, far])
    idx = src_ref[blocks:]

    def part_sum(s, c):
        near = spread_step(idx, s * shard + c * piece, piece, grad_ref[...])
        return most_ref[s, pl.ds(c * piece, piece)] + near

    sib_copies = []
    for slot, s in ((0, both), (1, sib)):
        loads[2 * slot].wait()
        for c in range(PIECES):
            part = pl.ds(c * piece, piece)
            to_sib[slot, part] = part_sum(s, c).astype(BF16)
            copy = pltpu.make_async_remote_copy(
                src_ref=to_sib.at[slot, part], dst_ref=from_sib.at[slot, part],
                send_sem=sib_send.at[slot, c], recv_sem=sib_recv.at[slot, c],
                device_id={"grp": sib}, device_id_type=MESH)
            copy.start()
            sib_copies.append(copy)
        if slot == 0:
            far_copies = []
            loads[1].wait()
            for c in range(PIECES):
                part = pl.ds(c * piece, piece)
                mine = part_sum(far, c)
                sib_copies[c].wait()
                to_far[part] = (mine + from_sib[0, part].astype(F32)).astype(BF16)
                copy = pltpu.make_async_remote_copy(
                    src_ref=to_far.at[part], dst_ref=from_far.at[part],
                    send_sem=far_send.at[c], recv_sem=far_recv.at[c],
                    device_id={"grp": far}, device_id_type=MESH)
                copy.start()
                far_copies.append(copy)
    loads[3].wait()
    for c in range(PIECES):
        part = pl.ds(c * piece, piece)
        mine = part_sum(g, c)
        sib_copies[PIECES + c].wait()
        out_ref[part] = mine + from_sib[1, part].astype(F32)
    for c in range(PIECES):
        part = pl.ds(c * piece, piece)
        far_copies[c].wait()
        out_ref[part] = out_ref[part] + from_far[part].astype(F32)


def spread_and_reduce(most, src, grad):
    shards, shard, depth = most.shape
    dma = pltpu.SemaphoreType.DMA
    return pl.pallas_call(
        reduce_kernel,
        out_shape=jax.ShapeDtypeStruct((shard, depth), F32),
        in_specs=[pl.BlockSpec(memory_space=pl.ANY), VMEM, VMEM],
        out_specs=VMEM,
        scratch_shapes=[
            pltpu.VMEM((shards, shard, depth), F32), dma((4,)),
            pltpu.VMEM((2, shard, depth), BF16), pltpu.VMEM((2, shard, depth), BF16),
            pltpu.VMEM((shard, depth), BF16), pltpu.VMEM((shard, depth), BF16),
            dma((2, PIECES)), dma((2, PIECES)), dma((PIECES,)), dma((PIECES,)),
        ],
        compiler_params=pltpu.CompilerParams(
            collective_id=1, has_side_effects=True, vmem_limit_bytes=LIMIT
        ),
    )(most, src, grad)


def on_device(emb, rel, round_key, edge_src, edge_dst, neg_idx, block_count):
    key = round_key[0]
    count_dom = lax.axis_size("dom")
    routes = [[(p, p ^ k) for p in range(count_dom)] for k in range(1, count_dom)]
    rel = rel[None]
    src, dst, neg, counts = edge_src[0, 0], edge_dst[0, 0], neg_idx[0, 0], block_count[0]
    shards, shard = lax.axis_size("grp"), emb.shape[1]
    table, mails = gather_table(emb[0], dst, neg, counts, count_dom)
    query_b = make_query(src, table, rel)
    mate = jnp.bitwise_xor(lax.axis_index("dom"), key)
    mail = lax.dynamic_index_in_dim(mails, mate, axis=0, keepdims=False)

    def out_way(route):
        def run(query, *rest):
            moved = lax.ppermute(query, "dom", route)
            return (moved,) + tuple(pick_and_score(*rest))

        return run

    query_in, near_grads, cand_in = lax.switch(
        key - 1, [out_way(r) for r in routes], query_b, counts, src, dst, neg, mail, table, rel
    )
    sgrad_in, cgrad_in = score_in(mail, query_in, cand_in, rel)

    def back_way(route):
        def run(sgrad, *rest):
            moved = lax.ppermute(sgrad, "dom", route)
            return moved, spread_most(*rest, shards, shard)

        return run

    sgrad_b, most = lax.switch(
        key - 1, [back_way(r) for r in routes], sgrad_in, src, dst, neg, mail, near_grads, cgrad_in
    )
    return spread_and_reduce(most, src, sgrad_b)[None]


def solution(mesh):
    return jax.shard_map(
        on_device,
        mesh=mesh,
        in_specs=(
            P("dom", "grp", None),
            P(),
            P(),
            P("grp", "dom", None, None),
            P("grp", "dom", None, None),
            P("grp", "dom", None, None),
            P("grp", "dom", None),
        ),
        out_specs=P("dom", "grp", None),
        check_vma=False,
    )
```

```python
import jax
import jax.numpy as jnp
from jax import lax
from jax.experimental import pallas as pl
from jax.experimental.pallas import tpu as pltpu
from jax.sharding import PartitionSpec as P

MESH = pl.DeviceIdType.MESH
F32 = jnp.float32
BF16 = jnp.bfloat16
STEP = 1024
EXACT = 256
PIECES = 4
VMEM = pl.BlockSpec(memory_space=pltpu.VMEM)
SMEM = pl.BlockSpec(memory_space=pltpu.SMEM)
LIMIT = 24 * 1024 * 1024


def grp_peers():
    g = lax.axis_index("grp")
    sib = g + 1 - 2 * lax.rem(g, 2)
    far = lax.rem(g + 2, 4)
    both = lax.rem(sib + 2, 4)
    return g, sib, far, both


def spread_step(idx_rows, base, tile, grads):
    line = jnp.concatenate([idx_rows[j : j + 1, :] for j in range(idx_rows.shape[0])], axis=1)
    parts = []
    for first in range(0, tile, EXACT):
        near = (line - (base + first)).astype(F32).astype(BF16)
        sub = lax.broadcasted_iota(jnp.int32, (EXACT, line.shape[1]), 0).astype(F32).astype(BF16)
        one = jnp.ones(sub.shape, BF16)
        parts.append(jnp.where(sub == near, one, jnp.zeros_like(one)))
    hot = jnp.concatenate(parts, axis=0) if len(parts) > 1 else parts[0]
    return jnp.dot(hot, grads, preferred_element_type=F32)


def load_wide(ref, at):
    return jnp.concatenate([ref[at, 0, :], ref[at, 1, :]], axis=1)


def pick_rows(idx_ref, first, blocks, table_ref, rows_ref, to):
    width = idx_ref.shape[1]
    unroll = 16

    @pl.loop(0, blocks * width // unroll)
    def _(i):
        b = lax.div(i, width // unroll)
        lane = lax.rem(i, width // unroll) * unroll
        got = [table_ref[idx_ref[first + b, lane + j]] for j in range(unroll)]
        for j in range(unroll):
            rows_ref[to + i * unroll + j] = got[j]


def score_block(query, cand, rel, live):
    width, depth = query.shape
    logits = lax.dot_general(query, cand, (((1,), (1,)), ((), ())), preferred_element_type=F32)
    top = jnp.max(logits, axis=1, keepdims=True)
    expd = jnp.exp(logits - top)
    probs = expd / jnp.sum(expd, axis=1, keepdims=True)
    row = lax.broadcasted_iota(jnp.int32, logits.shape, 0)
    col = lax.broadcasted_iota(jnp.int32, logits.shape, 1)
    weights = (probs - jnp.where(row == col, 1.0, 0.0)) * live
    weights_t = jnp.transpose(weights).astype(BF16)
    weights = weights.astype(BF16)
    grad_query = jnp.dot(weights, cand, preferred_element_type=F32)
    src_grad = (grad_query * rel * depth ** (-0.5)).astype(BF16)
    cand_grad = jnp.dot(weights_t, query, preferred_element_type=F32).astype(BF16)
    return src_grad, cand_grad


def gather_kernel(emb_ref, dst_ref, neg_ref, count_ref, wide_ref, mails_ref, table_ref, mail_ref,
                  own_send, own_recv, far_send, far_recv, fwd_send, fwd_recv, keep_sem,
                  mail_send, mail_recv):
    g, sib, far, both = grp_peers()
    d = lax.axis_index("dom")
    count_dom = mails_ref.shape[0]
    shard, depth = emb_ref.shape
    half = depth // 2
    piece = shard // PIECES
    blocks = dst_ref.shape[0] // 2
    barrier = pltpu.get_barrier_semaphore()
    for peer in (sib, far):
        pl.semaphore_signal(barrier, inc=1, device_id={"grp": peer}, device_id_type=MESH)
    for j in range(1, count_dom):
        pl.semaphore_signal(
            barrier, inc=1, device_id={"dom": lax.rem(d + j, count_dom)}, device_id_type=MESH
        )
    mail_ref[:blocks] = dst_ref[blocks:]
    mail_ref[blocks : 2 * blocks] = neg_ref[blocks:]
    mail_ref[2 * blocks :] = jnp.broadcast_to(count_ref[:, 1:2], (blocks, dst_ref.shape[1]))
    mails_ref[d] = mail_ref[...]
    keep = pltpu.make_async_copy(emb_ref, table_ref.at[g], keep_sem)
    keep.start()
    pl.semaphore_wait(barrier, 1 + count_dom)
    far_copies = []
    for c in range(PIECES):
        part = pl.ds(c * piece, piece)
        copy = pltpu.make_async_remote_copy(
            src_ref=emb_ref.at[part], dst_ref=table_ref.at[g, part],
            send_sem=far_send.at[c], recv_sem=far_recv.at[c],
            device_id={"grp": far}, device_id_type=MESH)
        copy.start()
        far_copies.append(copy)
    own = pltpu.make_async_remote_copy(
        src_ref=emb_ref, dst_ref=table_ref.at[g], send_sem=own_send, recv_sem=own_recv,
        device_id={"grp": sib}, device_id_type=MESH)
    own.start()
    mail_copies = []
    for j in range(1, count_dom):
        copy = pltpu.make_async_remote_copy(
            src_ref=mail_ref, dst_ref=mails_ref.at[d],
            send_sem=mail_send.at[j], recv_sem=mail_recv.at[j],
            device_id={"dom": lax.rem(d + j, count_dom)}, device_id_type=MESH)
        copy.start()
        mail_copies.append(copy)

    def widen(s, c):
        rows = table_ref[s, pl.ds(c * piece, piece)].astype(F32)
        at = pl.ds(pl.multiple_of(s * shard + c * piece, piece), piece)
        wide_ref[at, 0, :] = rows[:, :half]
        wide_ref[at, 1, :] = rows[:, half:]

    keep.wait()
    for c in range(PIECES):
        widen(g, c)
    own.wait()
    for c in range(PIECES):
        widen(sib, c)
    fwd_copies = []
    for c in range(PIECES):
        part = pl.ds(c * piece, piece)
        far_copies[c].wait()
        copy = pltpu.make_async_remote_copy(
            src_ref=table_ref.at[far, part], dst_ref=table_ref.at[far, part],
            send_sem=fwd_send.at[c], recv_sem=fwd_recv.at[c],
            device_id={"grp": sib}, device_id_type=MESH)
        copy.start()
        fwd_copies.append(copy)
        widen(far, c)
    for c in range(PIECES):
        fwd_copies[c].wait()
        widen(both, c)
    for copy in mail_copies:
        copy.wait()


def gather_table(emb, dst, neg, counts, count_dom):
    shard, depth = emb.shape
    dma = pltpu.SemaphoreType.DMA
    mail = (dst.shape[0] // 2 * 3, dst.shape[1])
    return pl.pallas_call(
        gather_kernel,
        out_shape=(
            jax.ShapeDtypeStruct((4 * shard, 2, depth // 2), F32),
            jax.ShapeDtypeStruct((count_dom,) + mail, jnp.int32),
        ),
        in_specs=[pl.BlockSpec(memory_space=pl.ANY)] + [VMEM] * 3,
        out_specs=(VMEM, VMEM),
        scratch_shapes=[
            pltpu.VMEM((4, shard, depth), BF16),
            pltpu.VMEM(mail, jnp.int32),
            dma, dma, dma((PIECES,)), dma((PIECES,)), dma((PIECES,)), dma((PIECES,)), dma,
            dma((count_dom,)), dma((count_dom,)),
        ],
        compiler_params=pltpu.CompilerParams(
            collective_id=0, has_side_effects=True, vmem_limit_bytes=LIMIT
        ),
    )(emb, dst, neg, counts)


def query_kernel(idx_ref, table_ref, rel_ref, query_ref, rows_ref):
    blocks = idx_ref.shape[0] // 2
    depth = query_ref.shape[1]
    pick_rows(idx_ref, blocks, blocks, table_ref, rows_ref, 0)
    for first in range(0, query_ref.shape[0], EXACT):
        at = pl.ds(first, EXACT)
        query_ref[at] = (load_wide(rows_ref, at) * rel_ref[...] * depth ** (-0.5)).astype(BF16)


def make_query(src, table, rel):
    entries = src.size // 2
    depth = rel.shape[1]
    return pl.pallas_call(
        query_kernel,
        out_shape=jax.ShapeDtypeStruct((entries, depth), BF16),
        in_specs=[SMEM, VMEM, VMEM],
        out_specs=VMEM,
        scratch_shapes=[pltpu.VMEM((entries, 2, depth // 2), F32)],
        compiler_params=pltpu.CompilerParams(vmem_limit_bytes=LIMIT),
    )(src, table, rel)


def pick_kernel(count_ref, src_ref, dst_ref, neg_ref, mail_ref, table_ref, rel_ref,
                grads_ref, cand_ref, rows_ref):
    width = src_ref.shape[1]
    blocks = src_ref.shape[0] // 2
    depth = cand_ref.shape[1]
    entries = blocks * width
    pick_rows(src_ref, 0, blocks, table_ref, rows_ref, 0)
    pick_rows(dst_ref, 0, blocks, table_ref, rows_ref, entries)
    pick_rows(neg_ref, 0, blocks, table_ref, rows_ref, 2 * entries)
    pick_rows(mail_ref, 0, 2 * blocks, table_ref, rows_ref, 3 * entries)

    @pl.loop(0, 2 * entries // EXACT)
    def _(i):
        at = pl.multiple_of(i * EXACT, EXACT)
        cand_ref[pl.ds(at, EXACT)] = load_wide(rows_ref, pl.ds(at + 3 * entries, EXACT)).astype(BF16)

    rel = rel_ref[...]

    @pl.loop(0, blocks // 4)
    def _(four):
        for b in [4 * four + j for j in range(4)]:
            at = pl.multiple_of(b * width, width)
            src_at = pl.ds(at, width)
            dst_at = pl.ds(at + entries, width)
            neg_at = pl.ds(at + 2 * entries, width)
            query = (load_wide(rows_ref, src_at) * rel * depth ** (-0.5)).astype(BF16)
            cand = jnp.concatenate(
                [load_wide(rows_ref, dst_at), load_wide(rows_ref, neg_at)], axis=0
            ).astype(BF16)
            live = jnp.where(b < count_ref[0, 0], 1.0, 0.0)
            src_grad, cand_grad = score_block(query, cand, rel, live)
            grads_ref[src_at] = src_grad
            grads_ref[dst_at] = cand_grad[:width]
            grads_ref[neg_at] = cand_grad[width:]


def pick_and_score(counts, src, dst, neg, mail, table, rel):
    entries = src.size // 2
    depth = rel.shape[1]
    return pl.pallas_call(
        pick_kernel,
        out_shape=(
            jax.ShapeDtypeStruct((3 * entries, depth), BF16),
            jax.ShapeDtypeStruct((2 * entries, depth), BF16),
        ),
        in_specs=[SMEM] * 5 + [VMEM] * 2,
        out_specs=(VMEM, VMEM),
        scratch_shapes=[pltpu.VMEM((5 * entries, 2, depth // 2), F32)],
        compiler_params=pltpu.CompilerParams(vmem_limit_bytes=LIMIT),
        cost_estimate=pl.CostEstimate(
            flops=10 * table.size * entries, bytes_accessed=30 * entries * depth, transcendentals=0
        ),
    )(counts, src, dst, neg, mail, table, rel)


def score_kernel(count_ref, query_ref, cand_ref, rel_ref, src_out, cand_out):
    rel = rel_ref[...]
    entries = query_ref.shape[0]
    width = count_ref.shape[1]
    blocks = entries // width

    @pl.loop(0, blocks // 4)
    def _(four):
        for b in [4 * four + j for j in range(4)]:
            at = pl.multiple_of(b * width, width)
            dst_at = pl.ds(at, width)
            neg_at = pl.ds(at + entries, width)
            cand = jnp.concatenate([cand_ref[dst_at], cand_ref[neg_at]], axis=0)
            live = jnp.where(b < count_ref[2 * blocks, 0], 1.0, 0.0)
            src_grad, cand_grad = score_block(query_ref[dst_at], cand, rel, live)
            src_out[dst_at] = src_grad
            cand_out[dst_at] = cand_grad[:width]
            cand_out[neg_at] = cand_grad[width:]


def score_in(count, query, cand, rel):
    return pl.pallas_call(
        score_kernel,
        out_shape=(
            jax.ShapeDtypeStruct(query.shape, BF16),
            jax.ShapeDtypeStruct(cand.shape, BF16),
        ),
        in_specs=[SMEM, VMEM, VMEM, VMEM],
        out_specs=(VMEM, VMEM),
        compiler_params=pltpu.CompilerParams(vmem_limit_bytes=LIMIT),
    )(count, query, cand, rel)


def spread_kernel(src_ref, dst_ref, neg_ref, mail_ref, near_ref, cand_ref, out_ref):
    shards, shard, depth = out_ref.shape
    blocks = src_ref.shape[0] // 2
    entries = blocks * src_ref.shape[1]
    tile = 512
    tiles = shard // tile

    @pl.loop(0, shards * tiles)
    def _(t):
        base = t * tile
        acc = jnp.zeros((tile, depth), F32)
        for i, ref in enumerate((src_ref, dst_ref, neg_ref)):
            grads = near_ref[i * entries : (i + 1) * entries]
            acc += spread_step(ref[:blocks], base, tile, grads)
        for i in range(2):
            grads = cand_ref[i * entries : (i + 1) * entries]
            acc += spread_step(mail_ref[i * blocks : (i + 1) * blocks], base, tile, grads)
        at = pl.ds(pl.multiple_of(lax.rem(t, tiles) * tile, tile), tile)
        out_ref[lax.div(t, tiles), at] = acc


def spread_most(src, dst, neg, mail, near, cand, shards, shard):
    entries, depth = near.shape[0] // 3, near.shape[1]
    return pl.pallas_call(
        spread_kernel,
        out_shape=jax.ShapeDtypeStruct((shards, shard, depth), F32),
        in_specs=[VMEM] * 6,
        out_specs=VMEM,
        compiler_params=pltpu.CompilerParams(vmem_limit_bytes=LIMIT),
        cost_estimate=pl.CostEstimate(
            flops=10 * entries * shards * shard * depth, bytes_accessed=40 * entries * depth,
            transcendentals=0,
        ),
    )(src, dst, neg, mail, near, cand)


def reduce_kernel(most_ref, src_ref, grad_ref, out_ref, to_sib, from_sib, to_far, from_far,
                  sib_send, sib_recv, far_send, far_recv):
    g, sib, far, both = grp_peers()
    shards, shard, depth = most_ref.shape
    piece = shard // PIECES
    blocks = src_ref.shape[0] // 2
    barrier = pltpu.get_barrier_semaphore()
    for peer in (sib, far):
        pl.semaphore_signal(barrier, inc=1, device_id={"grp": peer}, device_id_type=MESH)
    idx = src_ref[blocks:]
    sib_copies, far_copies = {}, {}

    def part_sum(s, c):
        near = spread_step(idx, s * shard + c * piece, piece, grad_ref[...])
        return most_ref[s, pl.ds(c * piece, piece)] + near

    def hold(slot, s, c):
        to_sib[slot, pl.ds(c * piece, piece)] = part_sum(s, c).astype(BF16)

    def post(slot, c):
        part = pl.ds(c * piece, piece)
        copy = pltpu.make_async_remote_copy(
            src_ref=to_sib.at[slot, part], dst_ref=from_sib.at[slot, part],
            send_sem=sib_send.at[slot, c], recv_sem=sib_recv.at[slot, c],
            device_id={"grp": sib}, device_id_type=MESH)
        copy.start()
        sib_copies[slot, c] = copy

    def cross(c):
        part = pl.ds(c * piece, piece)
        mine = part_sum(far, c)
        sib_copies[0, c].wait()
        to_far[part] = (mine + from_sib[0, part].astype(F32)).astype(BF16)
        copy = pltpu.make_async_remote_copy(
            src_ref=to_far.at[part], dst_ref=from_far.at[part],
            send_sem=far_send.at[c], recv_sem=far_recv.at[c],
            device_id={"grp": far}, device_id_type=MESH)
        copy.start()
        far_copies[c] = copy

    hold(0, both, 0)
    pl.semaphore_wait(barrier, 2)
    post(0, 0)
    for c in range(1, PIECES):
        hold(0, both, c)
        post(0, c)
        cross(c - 1)
    cross(PIECES - 1)
    for c in range(PIECES):
        hold(1, sib, c)
        post(1, c)
    for c in range(PIECES):
        part = pl.ds(c * piece, piece)
        mine = part_sum(g, c)
        sib_copies[1, c].wait()
        out_ref[part] = mine + from_sib[1, part].astype(F32)
    for c in range(PIECES):
        part = pl.ds(c * piece, piece)
        far_copies[c].wait()
        out_ref[part] = out_ref[part] + from_far[part].astype(F32)


def spread_and_reduce(most, src, grad):
    shards, shard, depth = most.shape
    dma = pltpu.SemaphoreType.DMA
    return pl.pallas_call(
        reduce_kernel,
        out_shape=jax.ShapeDtypeStruct((shard, depth), F32),
        in_specs=[VMEM] * 3,
        out_specs=VMEM,
        scratch_shapes=[
            pltpu.VMEM((2, shard, depth), BF16), pltpu.VMEM((2, shard, depth), BF16),
            pltpu.VMEM((shard, depth), BF16), pltpu.VMEM((shard, depth), BF16),
            dma((2, PIECES)), dma((2, PIECES)), dma((PIECES,)), dma((PIECES,)),
        ],
        compiler_params=pltpu.CompilerParams(
            collective_id=1, has_side_effects=True, vmem_limit_bytes=LIMIT
        ),
    )(most, src, grad)


def on_device(emb, rel, round_key, edge_src, edge_dst, neg_idx, block_count):
    key = round_key[0]
    count_dom = lax.axis_size("dom")
    routes = [[(p, p ^ k) for p in range(count_dom)] for k in range(1, count_dom)]
    rel = rel[None]
    src, dst, neg, counts = edge_src[0, 0], edge_dst[0, 0], neg_idx[0, 0], block_count[0]
    shards, shard = lax.axis_size("grp"), emb.shape[1]
    table, mails = gather_table(emb[0], dst, neg, counts, count_dom)
    query_b = make_query(src, table, rel)
    mate = jnp.bitwise_xor(lax.axis_index("dom"), key)
    mail = lax.dynamic_index_in_dim(mails, mate, axis=0, keepdims=False)

    def out_way(route):
        def run(query, *rest):
            moved = lax.ppermute(query, "dom", route)
            return (moved,) + tuple(pick_and_score(*rest))

        return run

    query_in, near_grads, cand_in = lax.switch(
        key - 1, [out_way(r) for r in routes], query_b, counts, src, dst, neg, mail, table, rel
    )
    sgrad_in, cgrad_in = score_in(mail, query_in, cand_in, rel)

    def back_way(route):
        def run(sgrad, *rest):
            moved = lax.ppermute(sgrad, "dom", route)
            return moved, spread_most(*rest, shards, shard)

        return run

    sgrad_b, most = lax.switch(
        key - 1, [back_way(r) for r in routes], sgrad_in, src, dst, neg, mail, near_grads, cgrad_in
    )
    return spread_and_reduce(most, src, sgrad_b)[None]


def solution(mesh):
    return jax.shard_map(
        on_device,
        mesh=mesh,
        in_specs=(
            P("dom", "grp", None),
            P(),
            P(),
            P("grp", "dom", None, None),
            P("grp", "dom", None, None),
            P("grp", "dom", None, None),
            P("grp", "dom", None),
        ),
        out_specs=P("dom", "grp", None),
        check_vma=False,
    )
```

```python
import jax
import jax.numpy as jnp
from jax import lax
from jax.experimental import pallas as pl
from jax.experimental.pallas import tpu as pltpu
from jax.sharding import PartitionSpec as P

MESH = pl.DeviceIdType.MESH
F32 = jnp.float32
BF16 = jnp.bfloat16
STEP = 1024
EXACT = 256
TILE = 512
PIECES = 4
VMEM = pl.BlockSpec(memory_space=pltpu.VMEM)
SMEM = pl.BlockSpec(memory_space=pltpu.SMEM)
HBM = pl.BlockSpec(memory_space=pltpu.HBM)
LIMIT = 24 * 1024 * 1024


def grp_peers():
    g = lax.axis_index("grp")
    sib = g + 1 - 2 * lax.rem(g, 2)
    far = lax.rem(g + 2, 4)
    both = lax.rem(sib + 2, 4)
    return g, sib, far, both


def spread_step(idx_rows, base, tile, grads):
    line = jnp.concatenate([idx_rows[j : j + 1, :] for j in range(idx_rows.shape[0])], axis=1)
    parts = []
    for first in range(0, tile, EXACT):
        near = (line - (base + first)).astype(F32).astype(BF16)
        sub = lax.broadcasted_iota(jnp.int32, (EXACT, line.shape[1]), 0).astype(F32).astype(BF16)
        one = jnp.ones(sub.shape, BF16)
        parts.append(jnp.where(sub == near, one, jnp.zeros_like(one)))
    hot = jnp.concatenate(parts, axis=0) if len(parts) > 1 else parts[0]
    return jnp.dot(hot, grads, preferred_element_type=F32)


def load_wide(ref, at):
    return jnp.concatenate([ref[at, 0, :], ref[at, 1, :]], axis=1)


def pick_rows(idx_ref, first, blocks, table_ref, rows_ref, to):
    width = idx_ref.shape[1]
    unroll = 16

    @pl.loop(0, blocks * width // unroll)
    def _(i):
        b = lax.div(i, width // unroll)
        lane = lax.rem(i, width // unroll) * unroll
        got = [table_ref[idx_ref[first + b, lane + j]] for j in range(unroll)]
        for j in range(unroll):
            rows_ref[to + i * unroll + j] = got[j]


def score_block(query, cand, rel, live):
    width, depth = query.shape
    logits = lax.dot_general(query, cand, (((1,), (1,)), ((), ())), preferred_element_type=F32)
    top = jnp.max(logits, axis=1, keepdims=True)
    expd = jnp.exp(logits - top)
    probs = expd / jnp.sum(expd, axis=1, keepdims=True)
    row = lax.broadcasted_iota(jnp.int32, logits.shape, 0)
    col = lax.broadcasted_iota(jnp.int32, logits.shape, 1)
    weights = (probs - jnp.where(row == col, 1.0, 0.0)) * live
    weights_t = jnp.transpose(weights).astype(BF16)
    weights = weights.astype(BF16)
    grad_query = jnp.dot(weights, cand, preferred_element_type=F32)
    src_grad = (grad_query * rel * depth ** (-0.5)).astype(BF16)
    cand_grad = jnp.dot(weights_t, query, preferred_element_type=F32).astype(BF16)
    return src_grad, cand_grad


def gather_kernel(emb_ref, dst_ref, neg_ref, count_ref, wide_ref, mails_ref, table_ref, mail_ref,
                  own_send, own_recv, far_send, far_recv, fwd_send, fwd_recv, keep_sem,
                  mail_send, mail_recv):
    g, sib, far, both = grp_peers()
    d = lax.axis_index("dom")
    count_dom = mails_ref.shape[0]
    shard, depth = emb_ref.shape
    half = depth // 2
    piece = shard // PIECES
    blocks = dst_ref.shape[0] // 2
    barrier = pltpu.get_barrier_semaphore()
    for peer in (sib, far):
        pl.semaphore_signal(barrier, inc=1, device_id={"grp": peer}, device_id_type=MESH)
    for j in range(1, count_dom):
        pl.semaphore_signal(
            barrier, inc=1, device_id={"dom": lax.rem(d + j, count_dom)}, device_id_type=MESH
        )
    mail_ref[:blocks] = dst_ref[blocks:]
    mail_ref[blocks : 2 * blocks] = neg_ref[blocks:]
    mail_ref[2 * blocks :] = jnp.broadcast_to(count_ref[:, 1:2], (blocks, dst_ref.shape[1]))
    mails_ref[d] = mail_ref[...]
    keep = pltpu.make_async_copy(emb_ref, table_ref.at[g], keep_sem)
    keep.start()
    pl.semaphore_wait(barrier, 1 + count_dom)
    far_copies = []
    for c in range(PIECES):
        part = pl.ds(c * piece, piece)
        copy = pltpu.make_async_remote_copy(
            src_ref=emb_ref.at[part], dst_ref=table_ref.at[g, part],
            send_sem=far_send.at[c], recv_sem=far_recv.at[c],
            device_id={"grp": far}, device_id_type=MESH)
        copy.start()
        far_copies.append(copy)
    own = pltpu.make_async_remote_copy(
        src_ref=emb_ref, dst_ref=table_ref.at[g], send_sem=own_send, recv_sem=own_recv,
        device_id={"grp": sib}, device_id_type=MESH)
    own.start()
    mail_copies = []
    for j in range(1, count_dom):
        copy = pltpu.make_async_remote_copy(
            src_ref=mail_ref, dst_ref=mails_ref.at[d],
            send_sem=mail_send.at[j], recv_sem=mail_recv.at[j],
            device_id={"dom": lax.rem(d + j, count_dom)}, device_id_type=MESH)
        copy.start()
        mail_copies.append(copy)

    def widen(s, c):
        rows = table_ref[s, pl.ds(c * piece, piece)].astype(F32)
        at = pl.ds(pl.multiple_of(s * shard + c * piece, piece), piece)
        wide_ref[at, 0, :] = rows[:, :half]
        wide_ref[at, 1, :] = rows[:, half:]

    keep.wait()
    for c in range(PIECES):
        widen(g, c)
    own.wait()
    for c in range(PIECES):
        widen(sib, c)
    fwd_copies = []
    for c in range(PIECES):
        part = pl.ds(c * piece, piece)
        far_copies[c].wait()
        copy = pltpu.make_async_remote_copy(
            src_ref=table_ref.at[far, part], dst_ref=table_ref.at[far, part],
            send_sem=fwd_send.at[c], recv_sem=fwd_recv.at[c],
            device_id={"grp": sib}, device_id_type=MESH)
        copy.start()
        fwd_copies.append(copy)
        widen(far, c)
    for c in range(PIECES):
        fwd_copies[c].wait()
        widen(both, c)
    for copy in mail_copies:
        copy.wait()


def gather_table(emb, dst, neg, counts, count_dom):
    shard, depth = emb.shape
    dma = pltpu.SemaphoreType.DMA
    mail = (dst.shape[0] // 2 * 3, dst.shape[1])
    return pl.pallas_call(
        gather_kernel,
        out_shape=(
            jax.ShapeDtypeStruct((4 * shard, 2, depth // 2), F32),
            jax.ShapeDtypeStruct((count_dom,) + mail, jnp.int32),
        ),
        in_specs=[HBM] + [VMEM] * 3,
        out_specs=(VMEM, VMEM),
        scratch_shapes=[
            pltpu.VMEM((4, shard, depth), BF16),
            pltpu.VMEM(mail, jnp.int32),
            dma, dma, dma((PIECES,)), dma((PIECES,)), dma((PIECES,)), dma((PIECES,)), dma,
            dma((count_dom,)), dma((count_dom,)),
        ],
        compiler_params=pltpu.CompilerParams(
            collective_id=0, has_side_effects=True, vmem_limit_bytes=LIMIT
        ),
    )(emb, dst, neg, counts)


def query_kernel(idx_ref, table_ref, rel_ref, query_ref, rows_ref):
    blocks = idx_ref.shape[0] // 2
    depth = query_ref.shape[1]
    pick_rows(idx_ref, blocks, blocks, table_ref, rows_ref, 0)
    for first in range(0, query_ref.shape[0], EXACT):
        at = pl.ds(first, EXACT)
        query_ref[at] = (load_wide(rows_ref, at) * rel_ref[...] * depth ** (-0.5)).astype(BF16)


def make_query(src, table, rel):
    entries = src.size // 2
    depth = rel.shape[1]
    return pl.pallas_call(
        query_kernel,
        out_shape=jax.ShapeDtypeStruct((entries, depth), BF16),
        in_specs=[SMEM, VMEM, VMEM],
        out_specs=VMEM,
        scratch_shapes=[pltpu.VMEM((entries, 2, depth // 2), F32)],
        compiler_params=pltpu.CompilerParams(vmem_limit_bytes=LIMIT),
    )(src, table, rel)


def pick_kernel(count_ref, src_ref, dst_ref, neg_ref, mail_ref, table_ref, rel_ref,
                grads_ref, cand_ref, rows_ref):
    width = src_ref.shape[1]
    blocks = src_ref.shape[0] // 2
    depth = cand_ref.shape[1]
    entries = blocks * width
    pick_rows(src_ref, 0, blocks, table_ref, rows_ref, 0)
    pick_rows(dst_ref, 0, blocks, table_ref, rows_ref, entries)
    pick_rows(neg_ref, 0, blocks, table_ref, rows_ref, 2 * entries)
    pick_rows(mail_ref, 0, 2 * blocks, table_ref, rows_ref, 3 * entries)

    @pl.loop(0, 2 * entries // EXACT)
    def _(i):
        at = pl.multiple_of(i * EXACT, EXACT)
        cand_ref[pl.ds(at, EXACT)] = load_wide(rows_ref, pl.ds(at + 3 * entries, EXACT)).astype(BF16)

    rel = rel_ref[...]

    @pl.loop(0, blocks // 4)
    def _(four):
        for b in [4 * four + j for j in range(4)]:
            at = pl.multiple_of(b * width, width)
            src_at = pl.ds(at, width)
            dst_at = pl.ds(at + entries, width)
            neg_at = pl.ds(at + 2 * entries, width)
            query = (load_wide(rows_ref, src_at) * rel * depth ** (-0.5)).astype(BF16)
            cand = jnp.concatenate(
                [load_wide(rows_ref, dst_at), load_wide(rows_ref, neg_at)], axis=0
            ).astype(BF16)
            live = jnp.where(b < count_ref[0, 0], 1.0, 0.0)
            src_grad, cand_grad = score_block(query, cand, rel, live)
            grads_ref[src_at] = src_grad
            grads_ref[dst_at] = cand_grad[:width]
            grads_ref[neg_at] = cand_grad[width:]


def pick_and_score(counts, src, dst, neg, mail, table, rel):
    entries = src.size // 2
    depth = rel.shape[1]
    return pl.pallas_call(
        pick_kernel,
        out_shape=(
            jax.ShapeDtypeStruct((3 * entries, depth), BF16),
            jax.ShapeDtypeStruct((2 * entries, depth), BF16),
        ),
        in_specs=[SMEM] * 5 + [VMEM] * 2,
        out_specs=(VMEM, VMEM),
        scratch_shapes=[pltpu.VMEM((5 * entries, 2, depth // 2), F32)],
        compiler_params=pltpu.CompilerParams(vmem_limit_bytes=LIMIT),
        cost_estimate=pl.CostEstimate(
            flops=10 * table.size * entries, bytes_accessed=30 * entries * depth, transcendentals=0
        ),
    )(counts, src, dst, neg, mail, table, rel)


def score_kernel(count_ref, query_ref, cand_ref, rel_ref, src_out, cand_out):
    rel = rel_ref[...]
    entries = query_ref.shape[0]
    width = count_ref.shape[1]
    blocks = entries // width

    @pl.loop(0, blocks // 4)
    def _(four):
        for b in [4 * four + j for j in range(4)]:
            at = pl.multiple_of(b * width, width)
            dst_at = pl.ds(at, width)
            neg_at = pl.ds(at + entries, width)
            cand = jnp.concatenate([cand_ref[dst_at], cand_ref[neg_at]], axis=0)
            live = jnp.where(b < count_ref[2 * blocks, 0], 1.0, 0.0)
            src_grad, cand_grad = score_block(query_ref[dst_at], cand, rel, live)
            src_out[dst_at] = src_grad
            cand_out[dst_at] = cand_grad[:width]
            cand_out[neg_at] = cand_grad[width:]


def score_in(count, query, cand, rel):
    return pl.pallas_call(
        score_kernel,
        out_shape=(
            jax.ShapeDtypeStruct(query.shape, BF16),
            jax.ShapeDtypeStruct(cand.shape, BF16),
        ),
        in_specs=[SMEM, VMEM, VMEM, VMEM],
        out_specs=(VMEM, VMEM),
        compiler_params=pltpu.CompilerParams(vmem_limit_bytes=LIMIT),
    )(count, query, cand, rel)


def spread_kernel(src_ref, dst_ref, neg_ref, mail_ref, near_ref, cand_ref, out_ref, tile_ref, tile_sem):
    shards, shard, depth = out_ref.shape
    blocks = src_ref.shape[0] // 2
    entries = blocks * src_ref.shape[1]
    tile = tile_ref.shape[1]
    tiles = shard // tile

    def send(t):
        at = pl.ds(pl.multiple_of(lax.rem(t, tiles) * tile, tile), tile)
        return pltpu.make_async_copy(tile_ref.at[t], out_ref.at[lax.div(t, tiles), at], tile_sem.at[t])

    @pl.loop(0, shards * tiles)
    def _(t):
        base = t * tile
        acc = jnp.zeros((tile, depth), F32)
        for i, ref in enumerate((src_ref, dst_ref, neg_ref)):
            grads = near_ref[i * entries : (i + 1) * entries]
            acc += spread_step(ref[:blocks], base, tile, grads)
        for i in range(2):
            grads = cand_ref[i * entries : (i + 1) * entries]
            acc += spread_step(mail_ref[i * blocks : (i + 1) * blocks], base, tile, grads)
        tile_ref[t] = acc
        send(t).start()

    for t in range(shards * tiles):
        send(t).wait()


def spread_most(src, dst, neg, mail, near, cand, shards, shard):
    entries, depth = near.shape[0] // 3, near.shape[1]
    return pl.pallas_call(
        spread_kernel,
        out_shape=jax.ShapeDtypeStruct((shards, shard, depth), F32),
        in_specs=[VMEM] * 6,
        out_specs=HBM,
        scratch_shapes=[
            pltpu.VMEM((shards * shard // TILE, TILE, depth), F32),
            pltpu.SemaphoreType.DMA((shards * shard // TILE,)),
        ],
        compiler_params=pltpu.CompilerParams(vmem_limit_bytes=LIMIT),
        cost_estimate=pl.CostEstimate(
            flops=10 * entries * shards * shard * depth, bytes_accessed=40 * entries * depth,
            transcendentals=0,
        ),
    )(src, dst, neg, mail, near, cand)


def reduce_kernel(total_ref, src_ref, grad_ref, out_ref, most_ref, most_sem, to_sib, from_sib, to_far, from_far,
                  sib_send, sib_recv, far_send, far_recv):
    g, sib, far, both = grp_peers()
    shards, shard, depth = most_ref.shape
    piece = shard // PIECES
    blocks = src_ref.shape[0] // 2
    barrier = pltpu.get_barrier_semaphore()
    for peer in (sib, far):
        pl.semaphore_signal(barrier, inc=1, device_id={"grp": peer}, device_id_type=MESH)
    idx = src_ref[blocks:]
    sib_copies, far_copies = {}, {}
    loads = []
    for i, s in enumerate((both, far, sib, g)):
        loads.append(pltpu.make_async_copy(total_ref.at[s], most_ref.at[s], most_sem.at[i]))
        loads[i].start()

    def part_sum(s, c):
        near = spread_step(idx, s * shard + c * piece, piece, grad_ref[...])
        return most_ref[s, pl.ds(c * piece, piece)] + near

    def hold(slot, s, c):
        to_sib[slot, pl.ds(c * piece, piece)] = part_sum(s, c).astype(BF16)

    def post(slot, c):
        part = pl.ds(c * piece, piece)
        copy = pltpu.make_async_remote_copy(
            src_ref=to_sib.at[slot, part], dst_ref=from_sib.at[slot, part],
            send_sem=sib_send.at[slot, c], recv_sem=sib_recv.at[slot, c],
            device_id={"grp": sib}, device_id_type=MESH)
        copy.start()
        sib_copies[slot, c] = copy

    def cross(c):
        part = pl.ds(c * piece, piece)
        mine = part_sum(far, c)
        sib_copies[0, c].wait()
        to_far[part] = (mine + from_sib[0, part].astype(F32)).astype(BF16)
        copy = pltpu.make_async_remote_copy(
            src_ref=to_far.at[part], dst_ref=from_far.at[part],
            send_sem=far_send.at[c], recv_sem=far_recv.at[c],
            device_id={"grp": far}, device_id_type=MESH)
        copy.start()
        far_copies[c] = copy

    loads[0].wait()
    hold(0, both, 0)
    pl.semaphore_wait(barrier, 2)
    post(0, 0)
    loads[1].wait()
    for c in range(1, PIECES):
        hold(0, both, c)
        post(0, c)
        cross(c - 1)
    cross(PIECES - 1)
    loads[2].wait()
    for c in range(PIECES):
        hold(1, sib, c)
        post(1, c)
    loads[3].wait()
    for c in range(PIECES):
        part = pl.ds(c * piece, piece)
        mine = part_sum(g, c)
        sib_copies[1, c].wait()
        out_ref[part] = mine + from_sib[1, part].astype(F32)
    for c in range(PIECES):
        part = pl.ds(c * piece, piece)
        far_copies[c].wait()
        out_ref[part] = out_ref[part] + from_far[part].astype(F32)


def spread_and_reduce(most, src, grad):
    shards, shard, depth = most.shape
    dma = pltpu.SemaphoreType.DMA
    return pl.pallas_call(
        reduce_kernel,
        out_shape=jax.ShapeDtypeStruct((shard, depth), F32),
        in_specs=[HBM, VMEM, VMEM],
        out_specs=VMEM,
        scratch_shapes=[
            pltpu.VMEM((shards, shard, depth), F32), dma((4,)),
            pltpu.VMEM((2, shard, depth), BF16), pltpu.VMEM((2, shard, depth), BF16),
            pltpu.VMEM((shard, depth), BF16), pltpu.VMEM((shard, depth), BF16),
            dma((2, PIECES)), dma((2, PIECES)), dma((PIECES,)), dma((PIECES,)),
        ],
        compiler_params=pltpu.CompilerParams(
            collective_id=1, has_side_effects=True, vmem_limit_bytes=LIMIT
        ),
    )(most, src, grad)


def on_device(emb, rel, round_key, edge_src, edge_dst, neg_idx, block_count):
    key = round_key[0]
    count_dom = lax.axis_size("dom")
    routes = [[(p, p ^ k) for p in range(count_dom)] for k in range(1, count_dom)]
    rel = rel[None]
    src, dst, neg, counts = edge_src[0, 0], edge_dst[0, 0], neg_idx[0, 0], block_count[0]
    shards, shard = lax.axis_size("grp"), emb.shape[1]
    table, mails = gather_table(emb[0], dst, neg, counts, count_dom)
    query_b = make_query(src, table, rel)
    mate = jnp.bitwise_xor(lax.axis_index("dom"), key)
    mail = lax.dynamic_index_in_dim(mails, mate, axis=0, keepdims=False)

    def out_way(route):
        def run(query, *rest):
            moved = lax.ppermute(query, "dom", route)
            return (moved,) + tuple(pick_and_score(*rest))

        return run

    query_in, near_grads, cand_in = lax.switch(
        key - 1, [out_way(r) for r in routes], query_b, counts, src, dst, neg, mail, table, rel
    )
    sgrad_in, cgrad_in = score_in(mail, query_in, cand_in, rel)

    def back_way(route):
        def run(sgrad, *rest):
            moved = lax.ppermute(sgrad, "dom", route)
            return moved, spread_most(*rest, shards, shard)

        return run

    sgrad_b, most = lax.switch(
        key - 1, [back_way(r) for r in routes], sgrad_in, src, dst, neg, mail, near_grads, cgrad_in
    )
    return spread_and_reduce(most, src, sgrad_b)[None]


def solution(mesh):
    return jax.shard_map(
        on_device,
        mesh=mesh,
        in_specs=(
            P("dom", "grp", None),
            P(),
            P(),
            P("grp", "dom", None, None),
            P("grp", "dom", None, None),
            P("grp", "dom", None, None),
            P("grp", "dom", None),
        ),
        out_specs=P("dom", "grp", None),
        check_vma=False,
    )
```
